1024 devices in a mesh: expert: 32 (over z), fsdp: 8 (over x, core), dp: 4 (over y).
Axes of the slice: x: 4, y: 4, z: 32, core: 2. Of those that a mesh axis runs over, the one named last changes fastest.
Arguments:
- out_grad: bfloat16 [20480, 2048], P(('expert', 'fsdp', 'dp')), may hold values from -0.59765625 to 0.59765625
- gates: float32 [20480, 8], P(('expert', 'fsdp', 'dp')), may hold values from 0.02 to 0.6
- routes: int32 [20480, 8], P(('expert', 'fsdp', 'dp')), may hold values from 0 to 63, all different within a row; in each aligned block of 20 rows (0 to 19, 20 to 39, ...) at most 7 rows name the same one
- hidden_acts: bfloat16 [64, 7168, 384], P('expert', ('fsdp', 'dp')), may hold values from -6 to 6
- w_down: bfloat16 [2048, 64, 384], P('fsdp', 'expert'), may hold values from -0.3125 to 0.3125
Outputs:
- hidden_grad: bfloat16 [64, 7168, 384], P('expert', ('fsdp', 'dp'))
- gate_grad: float32 [20480, 8], P(('expert', 'fsdp', 'dp'))
- weight_grad: float32 [2048, 64, 384], P('fsdp', 'expert')
The draws below stay inside these ranges and needn't reach their ends.
Inputs may be any that keep to these rules, and one draw needn't show every extreme that they name: `routes`: each token names 8 different experts. Among the 20 tokens of one device no expert is named by more than 7 of them, and in every draw some expert is named by exactly 7 tokens of some device.
All inputs are finite; a program needn't handle non-finite values.
Results may differ from the reference program's by a relative error of at most 0.018.
Values may be sent and summed in bfloat16 or wider, within the bound.
A program may use at most 32 MiB of HBM per device.

```python
import math
import jax
import jax.numpy as jnp
import numpy as np
from jax import lax

D = 2048
H = 384
TOP = 8
TOK_DEV = 20
EXPERTS = 64
SLOT = 7
TOKENS = 20480
N_EXPERT = 32
N_FSDP = 8
N_DP = 4
DEVICES = 1024


def levels(key, extent, shards, smallest, high):
    gain = 1.0
    for dim, shards_of in shards:
        draws = jax.random.uniform(jax.random.fold_in(jax.random.fold_in(key, 6), dim), (shards_of,), jnp.float32, smallest / len(shards), high / len(shards))
        gain = gain * jnp.repeat(jnp.exp(draws), extent[dim] // shards_of).reshape((-1,) + (1,) * (len(extent) - 1 - dim))
    return gain


def routed_block(rng, own, number, rows, count, top, bound, lean):
    order = jax.random.permutation(rng, count)
    crowded, common = load_shares(count, rows * top, bound, lean, True), load_shares(count, rows * top, bound, lean, False)
    places = jnp.arange(count)

    def named(sizes, turn):
        used = int((sizes > 0).sum())
        fixed = max(1, used // 4)
        moved = fixed + (places - fixed + turn * (used - fixed)) % max(1, count - fixed)
        return jnp.zeros((count,), jnp.int32).at[order[jnp.where(places < fixed, places, moved)]].set(jnp.asarray(sizes, jnp.int32))

    sizes = jnp.where(number % 4 == 0, named(crowded, number // 4), named(common, number - number // 4 - 1))
    mixed = jax.random.permutation(jax.random.fold_in(own, 3), count)
    donor, sink = mixed[0:count // 2 * 2:2], mixed[1:count // 2 * 2:2]
    room = jnp.minimum(sizes[donor] - 1, bound - sizes[sink]) // 2
    room = jnp.where((donor == order[0]) | (sink == order[0]) | (sizes[sink] == 0), 0, jnp.maximum(room, 0))
    moved = jax.random.randint(jax.random.fold_in(own, 4), (count // 2,), 0, 1 << 20) % (room + 1)
    sizes = sizes.at[donor].add(-moved).at[sink].add(moved)
    members = jnp.searchsorted(jnp.cumsum(sizes), jnp.arange(rows * top), side="right").astype(jnp.int32)
    listing = members.reshape(top, rows).T
    listing = listing[jax.random.permutation(jax.random.fold_in(own, 1), rows)]
    turn = jax.random.randint(jax.random.fold_in(own, 2), (rows, 1), 0, top)
    return jnp.take_along_axis(listing, (jnp.arange(top)[None, :] + turn) % top, axis=1)


def load_shares(count, total, most, slope, full):
    loads = [(1 << 20) // math.isqrt(grade ** slope) + 1 for grade in range(1, count + 1)]
    largest = most if full else min(most, max(-(-total // count), total * loads[0] // sum(loads)))
    least = 1 if total - largest >= count - 1 else 0
    holding, spare = [largest] + [least] * (count - 1), total - largest - least * (count - 1)
    while spare > 0:
        movable = [i for i in range(1, count) if holding[i] < largest] or [i for i in range(1, count) if holding[i] < most]
        mass, left = sum([loads[i] for i in movable]), spare
        for i in movable:
            addition = min(most - holding[i], max(1, left * loads[i] // mass), spare)
            holding[i] = holding[i] + addition
            spare = spare - addition
    return np.array(holding)


def noise(key, extent, scale, reach, cuts=(), held_as=jnp.bfloat16):
    drawn = scale * jax.random.normal(key, extent, jnp.float32)
    if cuts:
        drawn = drawn * levels(key, extent, cuts, -0.22, 0.18)
    return jnp.clip(drawn, -reach, reach).astype(held_as)


def setup_inputs(seed: int = 0) -> dict:
    streams_of = jax.random.split(jax.random.key(seed), 6)
    out_grad = noise(streams_of[0], (TOKENS, D), 0.1, 0.59765625, ((0, 1024),))
    gates = jnp.clip(jnp.exp(math.log(0.6) - 3.4011974 * jax.random.uniform(streams_of[1], (TOKENS, TOP), jnp.float32) ** levels(streams_of[1], (TOKENS, TOP), ((0, 1024),), -0.2, 0.2)), 0.02, 0.6)
    routes_keys = jax.random.split(jax.random.fold_in(streams_of[2], 1), TOKENS // TOK_DEV)
    routes_turns = jax.random.permutation(jax.random.fold_in(streams_of[2], 3), TOKENS // TOK_DEV)
    routes = jax.vmap(lambda own, number: routed_block(jax.random.fold_in(streams_of[2], 2), own, number, TOK_DEV, EXPERTS, TOP, SLOT, 2))(routes_keys, routes_turns).reshape((TOKENS, TOP))
    hidden_acts = noise(streams_of[3], (EXPERTS, DEVICES * SLOT, H), 1.0, 6.0, ((0, 32), (1, 32)))
    w_down = noise(streams_of[4], (D, EXPERTS, H), H ** -0.5, 0.3125, ((0, 8), (1, 32)))
    return {"out_grad": out_grad, "gates": gates, "routes": routes, "hidden_acts": hidden_acts, "w_down": w_down}


def reference(out_grad, gates, routes, hidden_acts, w_down):
    groups = N_FSDP * N_DP
    device_count = N_EXPERT * groups
    pairs = TOK_DEV * TOP
    experts = w_down.shape[1]
    blocks = routes.reshape(device_count, pairs)
    onehot = (blocks[:, :, None] == jnp.arange(experts, dtype=jnp.int32)[None, None, :]).astype(jnp.int32)
    rank_in = jnp.sum(onehot * (jnp.cumsum(onehot, axis=1) - 1), axis=2).astype(jnp.int32)
    block_ids = jnp.arange(device_count, dtype=jnp.int32)
    base_row = ((block_ids % groups) * N_EXPERT + block_ids // groups) * SLOT
    slot_row = (base_row[:, None] + rank_in).reshape(-1).astype(jnp.int32)
    flat_routes = routes.reshape(-1).astype(jnp.int32)
    token_ids = jnp.arange(flat_routes.shape[0], dtype=jnp.int32) // TOP
    row_total = hidden_acts.shape[1]
    token_table = jnp.full((experts, row_total), -1, jnp.int32).at[flat_routes, slot_row].set(token_ids)
    gate_half = lax.optimization_barrier(gates.astype(jnp.bfloat16))
    gate_table = jnp.zeros((experts, row_total), jnp.float32).at[flat_routes, slot_row].set(gate_half.reshape(-1).astype(jnp.float32))
    weights_by_expert = jnp.transpose(w_down, (1, 0, 2))

    def expert_step(inputs):
        token_row, gate_row, acts, weight = inputs
        is_live = token_row >= 0
        picked = out_grad[jnp.maximum(token_row, 0)]
        routed = jnp.where(is_live[:, None], picked, jnp.zeros((), out_grad.dtype))
        back_proj = jnp.dot(routed, weight, preferred_element_type=jnp.float32)
        hidden_grad = (gate_row[:, None] * back_proj).astype(jnp.bfloat16)
        expert_out = jnp.dot(acts, weight.T, preferred_element_type=jnp.float32)
        gate_sums = jnp.sum(routed.astype(jnp.float32) * expert_out, axis=1)
        scaled = (gate_row[:, None] * routed.astype(jnp.float32)).astype(jnp.bfloat16)
        scaled_groups = scaled.reshape(groups, -1, scaled.shape[1]).astype(jnp.float32)
        act_groups = acts.reshape(groups, -1, acts.shape[1]).astype(jnp.float32)
        partial_value = jnp.einsum("grd,grj->gdj", scaled_groups, act_groups, precision=lax.Precision.HIGHEST)
        partial_value = lax.optimization_barrier(partial_value.astype(jnp.bfloat16))
        weight_grad = jnp.sum(partial_value.astype(jnp.float32), axis=0)
        return hidden_grad, gate_sums, weight_grad

    hidden_grad, gate_sums, grads = lax.map(expert_step, (token_table, gate_table, hidden_acts, weights_by_expert))
    gate_grad = gate_sums[flat_routes, slot_row].reshape(routes.shape)
    weight_grad = jnp.transpose(grads, (1, 0, 2))
    return hidden_grad, gate_grad, weight_grad
```

```python
import functools

import jax
import jax.numpy as jnp
from jax import lax
from jax.experimental import pallas as pl
from jax.experimental.pallas import tpu as pltpu
from jax.sharding import PartitionSpec as P

MESH = pl.DeviceIdType.MESH
F32 = jnp.float32
BF16 = jnp.bfloat16
LANES = 128
RPAD = 8
CODE_SHIFT = 256.0
LAG = 3
PIECES = 3


def remote(src, dst, send, recv, where):
    return pltpu.make_async_remote_copy(
        src_ref=src, dst_ref=dst, send_sem=send, recv_sem=recv, device_id=where, device_id_type=MESH
    )


def kernel(
    n_e, n_x, n_p, tok,
    pre, hp, wt, code, hg_out, gg_out, wg_out,
    blk, xr, hidr, w2, spread, tgt, lanemask, p_send, p_recv, scaled_rows, gate_cols, acc,
    gs, gr, ws, wc, wd, wr, wag,
    x_send, x_recv, h_send, h_recv, w_send, w_recv, loc,
    z_send, z_recv, ps_send, ps_recv, g_send, g_recv, c_send, c_recv, r_send, r_recv, a_send, a_recv,
):
    me = lax.axis_index("expert")
    f = lax.axis_index("fsdp")
    p = lax.axis_index("dp")
    xi, core = f // 2, f % 2
    half = n_e // 2
    piece_rows = pre.shape[1] - 16
    og_rows = n_x * piece_rows
    blk_rows = og_rows + 16
    q_n = piece_rows // tok
    chunk = blk_rows // PIECES
    width = hp.shape[2]
    fs = wt.shape[1]
    rows_x = n_x * RPAD
    right, left = (me + 1) % n_e, (me + n_e - 1) % n_e

    def x_dev(t):
        return {"fsdp": t * 2 + core}

    other = {"fsdp": xi * 2 + 1 - core}

    barrier = pltpu.get_barrier_semaphore()

    @pl.loop(1, n_e)
    def _(o):
        pl.semaphore_signal(barrier, inc=1, device_id={"expert": (me + o) % n_e}, device_id_type=MESH)

    for o in range(1, n_x):
        pl.semaphore_signal(barrier, inc=1, device_id=x_dev((xi + o) % n_x), device_id_type=MESH)
    pl.semaphore_signal(barrier, inc=1, device_id=other, device_id_type=MESH)
    for o in range(1, n_p):
        pl.semaphore_signal(barrier, inc=1, device_id={"dp": (p + o) % n_p}, device_id_type=MESH)
    pl.semaphore_wait(barrier, (n_e - 1) + (n_x - 1) + 1 + (n_p - 1))

    def x_copy(o):
        t = (xi + o) % n_x
        return remote(pre.at[t], xr.at[xi], x_send.at[o - 1], x_recv.at[o - 1], x_dev(t))

    def h_copy(o):
        t = (xi + o) % n_x
        return remote(hp, hidr.at[xi], h_send.at[o - 1], h_recv.at[o - 1], x_dev(t))

    w_copy = remote(wt, w2.at[core], w_send, w_recv, other)
    own_w = pltpu.make_async_copy(wt, w2.at[core], loc.at[0])
    own_h = pltpu.make_async_copy(hp, hidr.at[xi], loc.at[1])
    own_x = pltpu.make_async_copy(pre.at[xi], xr.at[xi], loc.at[2])

    for o in range(1, n_x):
        x_copy(o).start()
    own_x.start()
    w_copy.start()
    for o in range(1, n_x):
        h_copy(o).start()
    own_w.start()
    own_h.start()

    k_tok = lax.broadcasted_iota(jnp.int32, spread.shape, 0)
    lane = lax.broadcasted_iota(jnp.int32, spread.shape, 1)
    token_of = lane // piece_rows * tok + lane % tok
    spread[...] = jnp.where((token_of == k_tok) & (lane < og_rows), 1.0, 0.0).astype(BF16)
    row = lax.broadcasted_iota(jnp.int32, tgt.shape, 0)
    col = lax.broadcasted_iota(jnp.int32, tgt.shape, 1)
    expert_row = me * 2 + row // rows_x
    tgt[...] = (expert_row * RPAD + row % RPAD).astype(F32) - CODE_SHIFT
    lanemask[...] = jnp.where(col // tok == row // RPAD % n_x, 1.0, 0.0)
    acc[...] = jnp.zeros_like(acc)
    gs[...] = jnp.zeros_like(gs)

    own_x.wait()
    for o in range(1, n_x):
        x_copy(o).wait_recv()
    table = jnp.zeros((16, LANES), F32)
    for x in range(n_x):
        blk[me, x * piece_rows : (x + 1) * piece_rows, :] = xr[x, :piece_rows, :]
        table = table + xr[x, piece_rows:, :].astype(F32)
    blk[me, og_rows:, :] = table.astype(BF16)

    def z_copy(way, step, c):
        slot = (me + n_e - step) % n_e if way == 0 else (me + step) % n_e
        ref = blk.at[slot, pl.ds(c * chunk, chunk), :]
        to = right if way == 0 else left
        return remote(ref, ref, z_send.at[way, step, c], z_recv.at[way, step, c], {"expert": to})

    def z_arrival(way, step, c):
        slot = (me + n_e - step - 1) % n_e if way == 0 else (me + step + 1) % n_e
        ref = blk.at[slot, pl.ds(c * chunk, chunk), :]
        to = right if way == 0 else left
        return remote(ref, ref, z_send.at[way, step, c], z_recv.at[way, step, c], {"expert": to})

    for c in range(PIECES):
        z_copy(0, 0, c).start()
        z_copy(1, 0, c).start()

    own_w.wait()
    w_copy.wait_recv()

    def block_rows(e, i, ab):
        routing = blk[e, og_rows:, :].astype(F32)
        codes, gates = routing[:8], routing[8:]
        want, mask = tgt[...], lanemask[...]
        hit = jnp.zeros(tgt.shape, F32)
        gate = jnp.zeros(tgt.shape, F32)
        for k in range(8):
            same = codes[k : k + 1, :] == want
            hit = jnp.where(same, 1.0, hit)
            gate = jnp.where(same, gates[k : k + 1, :], gate)
        gate_col = jnp.sum(gate * mask, axis=1, keepdims=True)
        gate_cols[i, ab] = jnp.broadcast_to(gate_col, tgt.shape)
        wide = jnp.dot((hit * mask).astype(BF16), spread[...], preferred_element_type=F32)
        q_of = lax.broadcasted_iota(jnp.int32, (1, blk_rows), 1) % piece_rows // tok
        pick = jnp.concatenate(
            [jnp.where(q_of == q, wide, 0.0).astype(BF16) for q in range(q_n)], axis=0
        )
        got = jnp.dot(pick, blk[e], preferred_element_type=F32)
        got = jnp.concatenate(
            [got[q * 2 * rows_x : (q + 1) * 2 * rows_x] for q in range(q_n)], axis=1
        )
        return got.astype(BF16), (got * gate_col).astype(BF16)

    def compute(i):
        ea, eb = (me + i) % n_e, (me + n_e - i - 1) % n_e
        rows_a, scaled_a = block_rows(ea, i, 0)
        rows_b, scaled_b = block_rows(eb, i, 1)
        parts = []
        for x in range(2):
            cut = slice(x * rows_x, (x + 1) * rows_x)
            scaled_rows[x, i, :rows_x, :] = scaled_a[cut]
            scaled_rows[x, i, rows_x:, :] = scaled_b[cut]
            lhs = jnp.concatenate([rows_a[cut], rows_b[cut]], axis=0)
            parts.append(
                jnp.dot(lhs[:, :fs], w2[0, x], preferred_element_type=F32)
                + jnp.dot(lhs[:, fs:], w2[1, x], preferred_element_type=F32)
            )
        for x in range(n_x):
            tiles = [
                parts[b][ab * rows_x + x * RPAD : ab * rows_x + (x + 1) * RPAD]
                for ab in range(2)
                for b in range(2)
            ]
            p_send[x, i] = jnp.concatenate(tiles, axis=0).astype(BF16)

    def p_copy(o, i):
        t = (xi + o) % n_x
        return remote(
            p_send.at[t, i], p_recv.at[xi, i], ps_send.at[o - 1, i], ps_recv.at[o - 1, i], x_dev(t)
        )

    def combine(i):
        for o in range(1, n_x):
            p_copy(o, i).wait_recv()
        total = p_send[xi, i].astype(F32)
        for o in range(1, n_x):
            total = total + p_recv[(xi + n_x - o) % n_x, i].astype(F32)
        for ab in range(2):
            e = (me + i) % n_e if ab == 0 else (me + n_e - i - 1) % n_e
            part = total[ab * 16 : (ab + 1) * 16]
            gate = jnp.concatenate(
                [gate_cols[i, ab, pl.ds(pl.multiple_of(x * rows_x + xi * RPAD, RPAD), RPAD), :] for x in range(2)],
                axis=0,
            )
            hg_out[e] = (gate[:, :1] * part).astype(BF16)
            grad = jnp.sum(part * hp[e].astype(F32), axis=1, keepdims=True)
            r16 = lax.broadcasted_iota(jnp.int32, (16, LANES), 0)
            l16 = lax.broadcasted_iota(jnp.int32, (16, LANES), 1)
            line = jnp.where(l16 == e % 8 * 16 + r16, grad, 0.0)
            gs[e // 8] += jnp.sum(line, axis=0, keepdims=True)

    def grad_step(j):
        for x in range(2):
            lhs, rhs = [], []
            for u in range(2):
                i = 2 * j + u
                lhs.append(scaled_rows[x, i])
                for ab in range(2):
                    e = (me + i) % n_e if ab == 0 else (me + n_e - i - 1) % n_e
                    for s in range(n_x):
                        rhs.append(hidr[s, e].astype(F32)[x * RPAD : (x + 1) * RPAD])
            lhs = jnp.concatenate(lhs, axis=0)
            rhs = jnp.concatenate(rhs, axis=0).astype(BF16)
            acc[x] += lax.dot_general(lhs, rhs, (((0,), (0,)), ((), ())), preferred_element_type=F32)

    @pl.loop(0, half)
    def _(i):
        for c in range(PIECES):
            z_arrival(0, i, c).wait_recv()

            @pl.when(i < half - 1)
            def _():
                z_copy(0, i + 1, c).start()

            @pl.when(i >= 1)
            def _():
                z_arrival(1, i - 1, c).wait_recv()

            @pl.when((i >= 1) & (i < half - 1))
            def _():
                z_copy(1, i, c).start()

        compute(i)
        for o in range(1, n_x):
            p_copy(o, i).start()

        @pl.when(i >= LAG)
        def _():
            combine(i - LAG)

        @pl.when(i == half // 2)
        def _():
            own_h.wait()
            for o in range(1, n_x):
                h_copy(o).wait_recv()

        @pl.when(i >= half // 2)
        def _():
            grad_step(i - half // 2)

    cut = fs // n_p
    for x in range(2):
        ws[x] = acc[x, pl.ds(pl.multiple_of((1 - core) * fs, fs), fs), :].astype(BF16)
    c_copy = remote(ws, wc, c_send, c_recv, other)
    c_copy.start()

    @pl.loop(half - LAG, half)
    def _(i):
        combine(i)

    gr[me] = gs[me // 8]

    def g_copy(o):
        t = (me + o) % n_e
        return remote(gs.at[t // 8], gr.at[me], g_send.at[o], g_recv.at[o], {"expert": t})

    @pl.loop(1, n_e)
    def _(o):
        g_copy(o).start()

    c_copy.wait_recv()

    def r_copy(o):
        t = (p + o) % n_p
        return remote(wd.at[t], wr.at[p], r_send.at[o - 1], r_recv.at[o - 1], {"dp": t})

    def summed(t, x):
        at = pl.multiple_of(core * fs + t * cut, cut)
        return acc[x, pl.ds(at, cut), :] + wc[x, pl.ds(pl.multiple_of(t * cut, cut), cut), :].astype(F32)

    for o in range(1, n_p):
        t = (p + o) % n_p
        for x in range(2):
            wd[t, x] = summed(t, x).astype(BF16)
        r_copy(o).start()

    @pl.loop(1, n_e)
    def _(o):
        g_copy(o).wait_recv()

    mine = [summed(p, x) for x in range(2)]
    for o in range(1, n_p):
        r_copy(o).wait_recv()
    for x in range(2):
        for o in range(1, n_p):
            mine[x] = mine[x] + wr[(p + n_p - o) % n_p, x].astype(F32)
        wag[p, x] = mine[x].astype(BF16)

    def a_copy(o):
        t = (p + o) % n_p
        return remote(wag.at[p], wag.at[p], a_send.at[o - 1], a_recv.at[o - 1], {"dp": t})

    def a_arrival(o):
        s = (p + n_p - o) % n_p
        return remote(
            wag.at[s], wag.at[s], a_send.at[o - 1], a_recv.at[o - 1], {"dp": (p + o) % n_p}
        )

    for o in range(1, n_p):
        a_copy(o).start()

    pairs = code[...]
    e_of = lax.broadcasted_iota(jnp.int32, (pairs.shape[0], n_e), 1)
    one = jnp.where(e_of == pairs // 16, 1.0, 0.0)
    got = jnp.dot(
        one, gr[:, 0, :], preferred_element_type=F32, precision=lax.Precision.HIGHEST
    )
    l_of = lax.broadcasted_iota(jnp.int32, got.shape, 1)
    gg_out[...] = jnp.sum(
        jnp.where(l_of == me % 8 * 16 + pairs % 16, got, 0.0), axis=1, keepdims=True
    )

    for o in range(1, n_p):
        a_arrival(o).wait_recv()
    for t in range(n_p):
        for x in range(2):
            wg_out[x, t * cut : (t + 1) * cut, :] = wag[t, x].astype(F32)

    for o in range(1, n_x):
        x_copy(o).wait_send()
        h_copy(o).wait_send()
    w_copy.wait_send()
    c_copy.wait_send()
    for o in range(1, n_p):
        r_copy(o).wait_send()
        a_copy(o).wait_send()

    @pl.loop(1, n_e)
    def _(o):
        g_copy(o).wait_send()

    @pl.loop(0, half)
    def _(i):
        for o in range(1, n_x):
            p_copy(o, i).wait_send()
        for c in range(PIECES):
            z_copy(0, i, c).wait_send()

            @pl.when(i < half - 1)
            def _():
                z_copy(1, i, c).wait_send()


def shards(n_e, n_x, n_p, out_grad, gates, routes, hidden_acts, w_down):
    tok, top = routes.shape
    exp_dev = w_down.shape[1]
    fs = w_down.shape[0]
    width = w_down.shape[2]
    slot = hidden_acts.shape[1] // n_e
    half = n_e // 2
    chip_cols = 2 * fs
    q_n = chip_cols // LANES
    piece_rows = q_n * tok
    blk_rows = n_x * piece_rows + 16
    rows_x = n_x * RPAD
    xi = lax.axis_index("fsdp") // 2

    earlier = jnp.arange(tok)[:, None] > jnp.arange(tok)[None, :]
    same = routes[:, :, None, None] == routes[None, None, :, :]
    rank = jnp.sum((same & earlier[:, None, :, None]).astype(jnp.int32), axis=(2, 3))
    code = routes * RPAD + rank
    table = jnp.concatenate(
        [(code.T.astype(F32) - CODE_SHIFT).astype(BF16), gates.T.astype(BF16)], axis=0
    )
    table = jnp.concatenate([table] * n_x, axis=1)
    table = jnp.pad(table, ((0, 0), (0, LANES - n_x * tok)))
    lane = jnp.arange(LANES, dtype=jnp.int32)
    table = jnp.where((lane // tok == xi)[None, :], table, jnp.zeros((), BF16))
    pieces = out_grad.reshape(tok, n_x, q_n, LANES).transpose(1, 2, 0, 3).reshape(n_x, piece_rows, LANES)
    pre = jnp.concatenate([pieces, jnp.broadcast_to(table[None], (n_x, 16, LANES))], axis=1)
    hp = hidden_acts.reshape(exp_dev, n_e, slot, width).transpose(1, 0, 2, 3)
    hp = jnp.pad(hp, ((0, 0), (0, 0), (0, RPAD - slot), (0, 0))).reshape(n_e, 2 * RPAD, width)
    wt = w_down.transpose(1, 0, 2)

    dma = pltpu.SemaphoreType.DMA
    vmem = pl.BlockSpec(memory_space=pltpu.VMEM)
    cut = fs // n_p
    hg, gg, wg = pl.pallas_call(
        functools.partial(kernel, n_e, n_x, n_p, tok),
        out_shape=(
            jax.ShapeDtypeStruct((n_e, 2 * RPAD, width), BF16),
            jax.ShapeDtypeStruct((tok * top, 1), F32),
            jax.ShapeDtypeStruct((exp_dev, fs, width), F32),
        ),
        in_specs=[vmem] * 4,
        out_specs=(vmem,) * 3,
        scratch_shapes=[
            pltpu.VMEM((n_e, blk_rows, LANES), BF16),
            pltpu.VMEM((n_x, piece_rows + 16, LANES), BF16),
            pltpu.VMEM((n_x, n_e, 2 * RPAD, width), BF16),
            pltpu.VMEM((2, exp_dev, fs, width), BF16),
            pltpu.VMEM((LANES, blk_rows), BF16),
            pltpu.VMEM((2 * rows_x, LANES), F32),
            pltpu.VMEM((2 * rows_x, LANES), F32),
            pltpu.VMEM((n_x, half, 4 * RPAD, width), BF16),
            pltpu.VMEM((n_x, half, 4 * RPAD, width), BF16),
            pltpu.VMEM((2, half, 2 * rows_x, chip_cols), BF16),
            pltpu.VMEM((half, 2, 2 * rows_x, LANES), F32),
            pltpu.VMEM((2, chip_cols, width), F32),
            pltpu.VMEM((n_e // 8, 1, LANES), F32),
            pltpu.VMEM((n_e, 1, LANES), F32),
            pltpu.VMEM((2, fs, width), BF16),
            pltpu.VMEM((2, fs, width), BF16),
            pltpu.VMEM((n_p, 2, cut, width), BF16),
            pltpu.VMEM((n_p, 2, cut, width), BF16),
            pltpu.VMEM((n_p, 2, cut, width), BF16),
            dma((n_x - 1,)), dma((n_x - 1,)), dma((n_x - 1,)), dma((n_x - 1,)), dma, dma, dma((3,)),
            dma((2, half, PIECES)), dma((2, half, PIECES)),
            dma((n_x - 1, half)), dma((n_x - 1, half)),
            dma((n_e,)), dma((n_e,)), dma, dma,
            dma((n_p - 1,)), dma((n_p - 1,)), dma((n_p - 1,)), dma((n_p - 1,)),
        ],
        compiler_params=pltpu.CompilerParams(
            collective_id=0, has_side_effects=True, vmem_limit_bytes=40 * 1024 * 1024
        ),
    )(pre, hp, wt, code.reshape(tok * top, 1))
    hg = hg.reshape(n_e, exp_dev, RPAD, width)[:, :, :slot].transpose(1, 0, 2, 3)
    return hg.reshape(exp_dev, n_e * slot, width), gg.reshape(tok, top), wg.transpose(1, 0, 2)


def solution(mesh):
    n_x = mesh.shape["fsdp"] // 2
    in_specs = (
        P(("expert", "fsdp", "dp"), None),
        P(("expert", "fsdp", "dp"), None),
        P(("expert", "fsdp", "dp"), None),
        P("expert", ("fsdp", "dp"), None),
        P("fsdp", "expert", None),
    )
    out_specs = (
        P("expert", ("fsdp", "dp"), None),
        P(("expert", "fsdp", "dp"), None),
        P("fsdp", "expert", None),
    )
    return jax.shard_map(
        functools.partial(shards, mesh.shape["expert"], n_x, mesh.shape["dp"]),
        mesh=mesh,
        in_specs=in_specs,
        out_specs=out_specs,
        check_vma=False,
    )
```

```python
import functools

import jax
import jax.numpy as jnp
from jax import lax
from jax.experimental import pallas as pl
from jax.experimental.pallas import tpu as pltpu
from jax.sharding import PartitionSpec as P

MESH = pl.DeviceIdType.MESH
F32 = jnp.float32
BF16 = jnp.bfloat16
LANES = 128
RPAD = 8
CODE_SHIFT = 256.0
PIECES = 3
JUMP = 6


def remote(src, dst, send, recv, where):
    return pltpu.make_async_remote_copy(
        src_ref=src, dst_ref=dst, send_sem=send, recv_sem=recv, device_id=where, device_id_type=MESH
    )


def kernel(
    n_e, n_x, n_p, tok,
    pre, routes, gates, hp, wt, hg_out, gg_out, wg_out,
    blk, xr, tile, tr, codes_own, hidr, w2, spread, tgt, lanemask, p_send, p_recv, scaled_rows, gate_cols, acc,
    gs, gr, ws, wc, wd, wr, wag,
    x_send, x_recv, t_send, t_recv, h_send, h_recv, w_send, w_recv, loc,
    z_send, z_recv, ps_send, ps_recv, g_send, g_recv, c_send, c_recv, r_send, r_recv, a_send, a_recv,
):
    me = lax.axis_index("expert")
    f = lax.axis_index("fsdp")
    p = lax.axis_index("dp")
    xi, core = f // 2, f % 2
    half = n_e // 2
    piece_rows = pre.shape[1]
    og_rows = n_x * piece_rows
    blk_rows = og_rows + 16
    q_n = piece_rows // tok
    chunk = blk_rows // PIECES
    width = hp.shape[2]
    fs = wt.shape[1]
    rows_x = n_x * RPAD

    def x_dev(t):
        return {"fsdp": t * 2 + core}

    other = {"fsdp": xi * 2 + 1 - core}

    barrier = pltpu.get_barrier_semaphore()

    for o in (1, n_e - 1, JUMP, n_e - JUMP):
        pl.semaphore_signal(barrier, inc=1, device_id={"expert": (me + o) % n_e}, device_id_type=MESH)
    for o in range(1, n_x):
        pl.semaphore_signal(barrier, inc=1, device_id=x_dev((xi + o) % n_x), device_id_type=MESH)
    pl.semaphore_signal(barrier, inc=1, device_id=other, device_id_type=MESH)
    for o in range(1, n_p):
        pl.semaphore_signal(barrier, inc=1, device_id={"dp": (p + o) % n_p}, device_id_type=MESH)
    pl.semaphore_wait(barrier, 4 + (n_x - 1) + 1 + (n_p - 1))

    def x_copy(o):
        t = (xi + o) % n_x
        return remote(pre.at[t], xr.at[xi], x_send.at[o - 1], x_recv.at[o - 1], x_dev(t))

    def t_copy(o):
        t = (xi + o) % n_x
        return remote(tile, tr.at[xi], t_send.at[o - 1], t_recv.at[o - 1], x_dev(t))

    def h_copy(o):
        t = (xi + o) % n_x
        return remote(hp, hidr.at[xi], h_send.at[o - 1], h_recv.at[o - 1], x_dev(t))

    w_copy = remote(wt, w2.at[core], w_send, w_recv, other)
    own_w = pltpu.make_async_copy(wt, w2.at[core], loc.at[0])
    own_h = pltpu.make_async_copy(hp, hidr.at[xi], loc.at[1])
    own_x = pltpu.make_async_copy(pre.at[xi], xr.at[xi], loc.at[2])

    for o in range(1, n_x):
        x_copy(o).start()
    own_x.start()
    w_copy.start()
    own_w.start()
    own_h.start()

    t_row = lax.broadcasted_iota(jnp.int32, (tok, LANES), 0)
    t_col = lax.broadcasted_iota(jnp.int32, (tok, LANES), 1)
    place = jnp.where(t_col == xi * tok + t_row, 1.0, 0.0)
    both = jnp.concatenate(
        [routes[...].astype(F32), gates[...].astype(BF16).astype(F32)], axis=0
    ).astype(BF16)
    placed = jnp.dot(both, place.astype(BF16), preferred_element_type=F32)
    own_lane = lax.broadcasted_iota(jnp.int32, (1, LANES), 1) // tok == xi
    expert = lax.broadcasted_iota(jnp.int32, (2 * n_e, LANES), 0).astype(F32)
    named = jnp.zeros((2 * n_e, LANES), F32)
    for k in range(8):
        named = jnp.where((placed[k : k + 1] == expert) & own_lane, 1.0, named)
    l_row = lax.broadcasted_iota(jnp.int32, (LANES, LANES), 0)
    l_col = lax.broadcasted_iota(jnp.int32, (LANES, LANES), 1)
    before = jnp.where(l_row < l_col, 1.0, 0.0).astype(BF16)
    count = jnp.dot(named.astype(BF16), before, preferred_element_type=F32)
    ranks = [
        jnp.sum(jnp.where(placed[k : k + 1] == expert, count, 0.0), axis=0, keepdims=True)
        for k in range(8)
    ]
    own_codes = placed[:8] * RPAD + jnp.concatenate(ranks, axis=0)
    codes_own[...] = own_codes
    tile[...] = jnp.concatenate(
        [jnp.where(own_lane, own_codes - CODE_SHIFT, 0.0), placed[8:]], axis=0
    ).astype(BF16)
    for o in range(1, n_x):
        t_copy(o).start()
    tr[xi] = tile[...]
    for o in range(1, n_x):
        h_copy(o).start()

    k_tok = lax.broadcasted_iota(jnp.int32, spread.shape, 0)
    lane = lax.broadcasted_iota(jnp.int32, spread.shape, 1)
    token_of = lane // piece_rows * tok + lane % tok
    spread[...] = jnp.where((token_of == k_tok) & (lane < og_rows), 1.0, 0.0).astype(BF16)
    row = lax.broadcasted_iota(jnp.int32, tgt.shape, 0)
    col = lax.broadcasted_iota(jnp.int32, tgt.shape, 1)
    expert_row = me * 2 + row // rows_x
    tgt[...] = (expert_row * RPAD + row % RPAD).astype(F32) - CODE_SHIFT
    lanemask[...] = jnp.where(col // tok == row // RPAD % n_x, 1.0, 0.0)
    acc[...] = jnp.zeros_like(acc)

    own_x.wait()
    for o in range(1, n_x):
        x_copy(o).wait_recv()
        t_copy(o).wait_recv()
    table = jnp.zeros((16, LANES), F32)
    for x in range(n_x):
        blk[me, x * piece_rows : (x + 1) * piece_rows, :] = xr[x]
        table = table + tr[x].astype(F32)
    blk[me, og_rows:, :] = table.astype(BF16)

    def hop(way, slot, dist, c, stride):
        ref = blk.at[slot, pl.ds(c * chunk, chunk), :]
        to = (me + stride) % n_e if way == 0 else (me + n_e - stride) % n_e
        return remote(ref, ref, z_send.at[way, dist - 1, c], z_recv.at[way, dist - 1, c], {"expert": to})

    def seen(way, dist):
        return (me + n_e - dist) % n_e if way == 0 else (me + dist) % n_e

    def order(i):
        mid = jnp.where(i % 2 == 0, JUMP - 1 + i // 2, (i + 3) // 2)
        return jnp.where((i < 2) | (i >= 2 * JUMP - 4), i + 1, mid)

    for c in range(PIECES):
        for way in range(2):
            hop(way, me, 1, c, 1).start()
    for c in range(PIECES):
        for way in range(2):
            hop(way, me, JUMP, c, JUMP).start()

    def pass_on(way, dist, c, last):
        hop(way, seen(way, dist), dist, c, 1).wait_recv()

        @pl.when((dist != JUMP - 1) & (dist != last))
        def _():
            hop(way, seen(way, dist), dist + 1, c, 1).start()

    def pair(i):
        far = jnp.where(i >= 1, order(jnp.maximum(i - 1, 0)), 0)
        return seen(1, far), seen(0, order(i))

    own_w.wait()
    w_copy.wait_recv()

    def block_rows(e, i, ab):
        routing = blk[e, og_rows:, :].astype(F32)
        codes, gates = routing[:8], routing[8:]
        want, mask = tgt[...], lanemask[...]
        hit = jnp.zeros(tgt.shape, F32)
        gate = jnp.zeros(tgt.shape, F32)
        for k in range(8):
            same = codes[k : k + 1, :] == want
            hit = jnp.where(same, 1.0, hit)
            gate = jnp.where(same, gates[k : k + 1, :], gate)
        gate_col = jnp.sum(gate * mask, axis=1, keepdims=True)
        gate_cols[i, ab] = jnp.broadcast_to(gate_col, tgt.shape)
        wide = jnp.dot((hit * mask).astype(BF16), spread[...], preferred_element_type=F32)
        q_of = lax.broadcasted_iota(jnp.int32, (1, blk_rows), 1) % piece_rows // tok
        pick = jnp.concatenate(
            [jnp.where(q_of == q, wide, 0.0).astype(BF16) for q in range(q_n)], axis=0
        )
        got = jnp.dot(pick, blk[e], preferred_element_type=F32)
        got = jnp.concatenate(
            [got[q * 2 * rows_x : (q + 1) * 2 * rows_x] for q in range(q_n)], axis=1
        )
        return got.astype(BF16), (got * gate_col).astype(BF16)

    def compute(i):
        ea, eb = pair(i)
        rows_a, scaled_a = block_rows(ea, i, 0)
        rows_b, scaled_b = block_rows(eb, i, 1)
        parts = []
        for x in range(2):
            cut = slice(x * rows_x, (x + 1) * rows_x)
            scaled_rows[x, i, :rows_x, :] = scaled_a[cut]
            scaled_rows[x, i, rows_x:, :] = scaled_b[cut]
            lhs = jnp.concatenate([rows_a[cut], rows_b[cut]], axis=0)
            parts.append(
                jnp.dot(lhs[:, :fs], w2[0, x], preferred_element_type=F32)
                + jnp.dot(lhs[:, fs:], w2[1, x], preferred_element_type=F32)
            )
        for x in range(n_x):
            tiles = [
                parts[b][ab * rows_x + x * RPAD : ab * rows_x + (x + 1) * RPAD]
                for ab in range(2)
                for b in range(2)
            ]
            p_send[x, i] = jnp.concatenate(tiles, axis=0).astype(BF16)

    def p_copy(o, i):
        t = (xi + o) % n_x
        return remote(
            p_send.at[t, i], p_recv.at[xi, i], ps_send.at[o - 1, i], ps_recv.at[o - 1, i], x_dev(t)
        )

    def g_copy(o):
        t = (me + o) % n_e
        return remote(gs.at[t], gr.at[me], g_send.at[o], g_recv.at[o], {"expert": t})

    def combine(i):
        for o in range(1, n_x):
            p_copy(o, i).wait_recv()
        total = p_send[xi, i].astype(F32)
        for o in range(1, n_x):
            total = total + p_recv[(xi + n_x - o) % n_x, i].astype(F32)
        for ab in range(2):
            e = pair(i)[ab]
            part = total[ab * 16 : (ab + 1) * 16]
            gate = jnp.concatenate(
                [gate_cols[i, ab, pl.ds(pl.multiple_of(x * rows_x + xi * RPAD, RPAD), RPAD), :] for x in range(2)],
                axis=0,
            )
            hg_out[e] = (gate[:, :1] * part).astype(BF16)
            grad = jnp.sum(part * hp[e].astype(F32), axis=1, keepdims=True)
            r16 = lax.broadcasted_iota(jnp.int32, (16, LANES), 0)
            l16 = lax.broadcasted_iota(jnp.int32, (16, LANES), 1)
            line = jnp.where(l16 == r16, grad, 0.0)
            gs[e] = jnp.sum(line, axis=0, keepdims=True)

        g_copy(n_e - order(i)).start()

        @pl.when(i >= 1)
        def _():
            g_copy(order(jnp.maximum(i - 1, 0))).start()

    def grad_step(j):
        for x in range(2):
            lhs, rhs = [], []
            for u in range(2):
                i = 2 * j + u
                lhs.append(scaled_rows[x, i])
                for ab in range(2):
                    e = pair(i)[ab]
                    for s in range(n_x):
                        rhs.append(hidr[s, e].astype(F32)[x * RPAD : (x + 1) * RPAD])
            lhs = jnp.concatenate(lhs, axis=0)
            rhs = jnp.concatenate(rhs, axis=0).astype(BF16)
            acc[x] += lax.dot_general(lhs, rhs, (((0,), (0,)), ((), ())), preferred_element_type=F32)

    @pl.loop(0, half)
    def _(i):
        for c in range(PIECES):
            pass_on(0, order(i), c, half)

            @pl.when(i >= 1)
            def _():
                pass_on(1, order(jnp.maximum(i - 1, 0)), c, half - 1)

        compute(i)
        for o in range(1, n_x):
            p_copy(o, i).start()

        @pl.when(i >= half // 2)
        def _():
            combine(i - half // 2)

        @pl.when(i >= 3 * half // 4)
        def _():
            combine(i - half // 4)

        @pl.when(i == half // 2)
        def _():
            own_h.wait()
            for o in range(1, n_x):
                h_copy(o).wait_recv()

        @pl.when(i >= half // 2)
        def _():
            grad_step(i - half // 2)

    cut = fs // n_p

    def c_copy(x):
        return remote(ws.at[x], wc.at[x], c_send.at[x], c_recv.at[x], other)

    def r_copy(o, x):
        t = (p + o) % n_p
        return remote(wd.at[t, x], wr.at[p, x], r_send.at[o - 1, x], r_recv.at[o - 1, x], {"dp": t})

    def a_copy(o, x, src):
        at = wag.at[src, x]
        return remote(at, at, a_send.at[o - 1, x], a_recv.at[o - 1, x], {"dp": (p + o) % n_p})

    def summed(t, x):
        at = pl.multiple_of(core * fs + t * cut, cut)
        return acc[x, pl.ds(at, cut), :] + wc[x, pl.ds(pl.multiple_of(t * cut, cut), cut), :].astype(F32)

    for x in range(2):
        ws[x] = acc[x, pl.ds(pl.multiple_of((1 - core) * fs, fs), fs), :].astype(BF16)
        c_copy(x).start()
    for x in range(2):
        c_copy(x).wait_recv()
        for o in range(1, n_p):
            t = (p + o) % n_p
            wd[t, x] = summed(t, x).astype(BF16)
            r_copy(o, x).start()

    @pl.loop(3 * half // 4, half)
    def _(i):
        combine(i)

    gr[me] = gs[me]
    for x in range(2):
        mine = summed(p, x)
        for o in range(1, n_p):
            r_copy(o, x).wait_recv()
            mine = mine + wr[(p + n_p - o) % n_p, x].astype(F32)
        wag[p, x] = mine.astype(BF16)
        for o in range(1, n_p):
            a_copy(o, x, p).start()

    @pl.loop(1, n_e)
    def _(o):
        g_copy(o).wait_recv()

    own = codes_own[...].astype(jnp.int32)
    e_of = lax.broadcasted_iota(jnp.int32, (n_e, LANES), 0)
    one = jnp.concatenate(
        [jnp.where(e_of == own[k : k + 1] // 16, 1.0, 0.0) for k in range(8)], axis=1
    )
    got = lax.dot_general(
        gr[:, 0, :], one, (((0,), (0,)), ((), ())),
        preferred_element_type=F32, precision=lax.Precision.HIGHEST,
    )[:16]
    s_of = lax.broadcasted_iota(jnp.int32, (16, LANES), 0)
    lines = [
        jnp.sum(
            jnp.where(s_of == own[k : k + 1] % 16, got[:, k * LANES : (k + 1) * LANES], 0.0),
            axis=0, keepdims=True,
        )
        for k in range(8)
    ]
    gg_out[...] = lax.dot_general(
        jnp.concatenate(lines, axis=0), place, (((1,), (1,)), ((), ())),
        preferred_element_type=F32, precision=lax.Precision.HIGHEST,
    )

    for x in range(2):
        wg_out[x, pl.ds(pl.multiple_of(p * cut, cut), cut), :] = wag[p, x].astype(F32)
        for o in range(1, n_p):
            src = (p + n_p - o) % n_p
            a_copy(o, x, src).wait_recv()
            wg_out[x, pl.ds(pl.multiple_of(src * cut, cut), cut), :] = wag[src, x].astype(F32)

    for o in range(1, n_x):
        x_copy(o).wait_send()
        t_copy(o).wait_send()
        h_copy(o).wait_send()
    w_copy.wait_send()
    for x in range(2):
        c_copy(x).wait_send()
        for o in range(1, n_p):
            r_copy(o, x).wait_send()
            a_copy(o, x, p).wait_send()

    @pl.loop(1, n_e)
    def _(o):
        g_copy(o).wait_send()

    @pl.loop(0, half)
    def _(i):
        for o in range(1, n_x):
            p_copy(o, i).wait_send()
        for c in range(PIECES):
            hop(0, me, i + 1, c, 1).wait_send()

            @pl.when(i < half - 1)
            def _():
                hop(1, me, i + 1, c, 1).wait_send()


def shards(n_e, n_x, n_p, out_grad, gates, routes, hidden_acts, w_down):
    tok, top = routes.shape
    exp_dev = w_down.shape[1]
    fs = w_down.shape[0]
    width = w_down.shape[2]
    slot = hidden_acts.shape[1] // n_e
    half = n_e // 2
    chip_cols = 2 * fs
    q_n = chip_cols // LANES
    piece_rows = q_n * tok
    blk_rows = n_x * piece_rows + 16
    rows_x = n_x * RPAD

    pre = out_grad.reshape(tok, n_x, q_n, LANES).transpose(1, 2, 0, 3).reshape(n_x, piece_rows, LANES)
    hp = hidden_acts.reshape(exp_dev, n_e, slot, width).transpose(1, 0, 2, 3)
    hp = jnp.pad(hp, ((0, 0), (0, 0), (0, RPAD - slot), (0, 0))).reshape(n_e, 2 * RPAD, width)
    wt = w_down.transpose(1, 0, 2)

    dma = pltpu.SemaphoreType.DMA
    vmem = pl.BlockSpec(memory_space=pltpu.VMEM)
    cut = fs // n_p
    hg, gg, wg = pl.pallas_call(
        functools.partial(kernel, n_e, n_x, n_p, tok),
        out_shape=(
            jax.ShapeDtypeStruct((n_e, 2 * RPAD, width), BF16),
            jax.ShapeDtypeStruct((top, tok), F32),
            jax.ShapeDtypeStruct((exp_dev, fs, width), F32),
        ),
        in_specs=[vmem] * 5,
        out_specs=(vmem,) * 3,
        scratch_shapes=[
            pltpu.VMEM((n_e, blk_rows, LANES), BF16),
            pltpu.VMEM((n_x, piece_rows, LANES), BF16),
            pltpu.VMEM((16, LANES), BF16),
            pltpu.VMEM((n_x, 16, LANES), BF16),
            pltpu.VMEM((8, LANES), F32),
            pltpu.VMEM((n_x, n_e, 2 * RPAD, width), BF16),
            pltpu.VMEM((2, exp_dev, fs, width), BF16),
            pltpu.VMEM((LANES, blk_rows), BF16),
            pltpu.VMEM((2 * rows_x, LANES), F32),
            pltpu.VMEM((2 * rows_x, LANES), F32),
            pltpu.VMEM((n_x, half, 4 * RPAD, width), BF16),
            pltpu.VMEM((n_x, half, 4 * RPAD, width), BF16),
            pltpu.VMEM((2, half, 2 * rows_x, chip_cols), BF16),
            pltpu.VMEM((half, 2, 2 * rows_x, LANES), F32),
            pltpu.VMEM((2, chip_cols, width), F32),
            pltpu.VMEM((n_e, 1, LANES), F32),
            pltpu.VMEM((n_e, 1, LANES), F32),
            pltpu.VMEM((2, fs, width), BF16),
            pltpu.VMEM((2, fs, width), BF16),
            pltpu.VMEM((n_p, 2, cut, width), BF16),
            pltpu.VMEM((n_p, 2, cut, width), BF16),
            pltpu.VMEM((n_p, 2, cut, width), BF16),
            dma((n_x - 1,)), dma((n_x - 1,)), dma((n_x - 1,)), dma((n_x - 1,)), dma((n_x - 1,)), dma((n_x - 1,)),
            dma, dma, dma((3,)),
            dma((2, half, PIECES)), dma((2, half, PIECES)),
            dma((n_x - 1, half)), dma((n_x - 1, half)),
            dma((n_e,)), dma((n_e,)), dma((2,)), dma((2,)),
            dma((n_p - 1, 2)), dma((n_p - 1, 2)), dma((n_p - 1, 2)), dma((n_p - 1, 2)),
        ],
        compiler_params=pltpu.CompilerParams(
            collective_id=0, has_side_effects=True, vmem_limit_bytes=40 * 1024 * 1024
        ),
    )(pre, routes.T, gates.T, hp, wt)
    hg = hg.reshape(n_e, exp_dev, RPAD, width)[:, :, :slot].transpose(1, 0, 2, 3)
    return hg.reshape(exp_dev, n_e * slot, width), gg.T, wg.transpose(1, 0, 2)


def solution(mesh):
    n_x = mesh.shape["fsdp"] // 2
    in_specs = (
        P(("expert", "fsdp", "dp"), None),
        P(("expert", "fsdp", "dp"), None),
        P(("expert", "fsdp", "dp"), None),
        P("expert", ("fsdp", "dp"), None),
        P("fsdp", "expert", None),
    )
    out_specs = (
        P("expert", ("fsdp", "dp"), None),
        P(("expert", "fsdp", "dp"), None),
        P("fsdp", "expert", None),
    )
    return jax.shard_map(
        functools.partial(shards, mesh.shape["expert"], n_x, mesh.shape["dp"]),
        mesh=mesh,
        in_specs=in_specs,
        out_specs=out_specs,
        check_vma=False,
    )
```

```python
import functools

import jax
import jax.numpy as jnp
from jax import lax
from jax.experimental import pallas as pl
from jax.experimental.pallas import tpu as pltpu
from jax.sharding import PartitionSpec as P

MESH = pl.DeviceIdType.MESH
F32 = jnp.float32
BF16 = jnp.bfloat16
LANES = 128
RPAD = 8
CODE_SHIFT = 256.0
PIECES = 3
JUMP = 4


def remote(src, dst, send, recv, where):
    return pltpu.make_async_remote_copy(
        src_ref=src, dst_ref=dst, send_sem=send, recv_sem=recv, device_id=where, device_id_type=MESH
    )


def wrap(v, n):
    return jnp.where(v >= n, v - n, v)


def kernel(
    n_e, n_x, n_p, tok,
    pre, routes, gates, hp, wt, hg_out, gg_out, wg_out,
    blk, xr, tile, tr, codes_own, hidr, w2, spread, tgt, lanemask, p_send, p_recv, scaled_rows, gate_cols, acc,
    gs, gr, ws, wc, wd, wr, wag,
    x_send, x_recv, t_send, t_recv, h_send, h_recv, w_send, w_recv, loc,
    z_send, z_recv, d_send, d_recv, o_send, o_recv, ps_send, ps_recv, g_send, g_recv, c_send, c_recv, r_send, r_recv, a_send, a_recv,
):
    me = lax.axis_index("expert")
    f = lax.axis_index("fsdp")
    p = lax.axis_index("dp")
    xi, core = f // 2, f % 2
    half = n_e // 2
    piece_rows = pre.shape[1]
    og_rows = n_x * piece_rows
    blk_rows = og_rows + 16
    q_n = piece_rows // tok
    chunk = blk_rows // PIECES
    width = hp.shape[2]
    fs = wt.shape[1]
    rows_x = n_x * RPAD

    def x_dev(t):
        return {"fsdp": t * 2 + core}

    other = {"fsdp": xi * 2 + 1 - core}

    barrier = pltpu.get_barrier_semaphore()

    for o in (1, n_e - 1, JUMP, n_e - JUMP):
        pl.semaphore_signal(barrier, inc=1, device_id={"expert": wrap(me + o, n_e)}, device_id_type=MESH)
    for o in range(1, n_x):
        pl.semaphore_signal(barrier, inc=1, device_id=x_dev(wrap(xi + o, n_x)), device_id_type=MESH)
    pl.semaphore_signal(barrier, inc=1, device_id=other, device_id_type=MESH)
    for o in range(1, n_p):
        pl.semaphore_signal(barrier, inc=1, device_id={"dp": wrap(p + o, n_p)}, device_id_type=MESH)
    pl.semaphore_wait(barrier, 4 + (n_x - 1) + 1 + (n_p - 1))

    def x_copy(o):
        t = wrap(xi + o, n_x)
        return remote(pre.at[t], xr.at[xi], x_send.at[o - 1], x_recv.at[o - 1], x_dev(t))

    def t_copy(o):
        t = wrap(xi + o, n_x)
        return remote(tile, tr.at[xi], t_send.at[o - 1], t_recv.at[o - 1], x_dev(t))

    def h_copy(o):
        t = wrap(xi + o, n_x)
        return remote(hp, hidr.at[xi], h_send.at[o - 1], h_recv.at[o - 1], x_dev(t))

    w_copy = remote(wt, w2.at[core], w_send, w_recv, other)
    own_w = pltpu.make_async_copy(wt, w2.at[core], loc.at[0])
    own_h = pltpu.make_async_copy(hp, hidr.at[xi], loc.at[1])
    own_x = pltpu.make_async_copy(pre.at[xi], xr.at[xi], loc.at[2])

    for o in range(1, n_x):
        x_copy(o).start()
    own_x.start()
    w_copy.start()
    own_w.start()
    own_h.start()

    t_row = lax.broadcasted_iota(jnp.int32, (tok, LANES), 0)
    t_col = lax.broadcasted_iota(jnp.int32, (tok, LANES), 1)
    place = jnp.where(t_col == xi * tok + t_row, 1.0, 0.0)
    both = jnp.concatenate(
        [routes[...].astype(F32), gates[...].astype(BF16).astype(F32)], axis=0
    ).astype(BF16)
    placed = jnp.dot(both, place.astype(BF16), preferred_element_type=F32)
    own_lane = lax.broadcasted_iota(jnp.int32, (1, LANES), 1) // tok == xi
    expert = lax.broadcasted_iota(jnp.int32, (2 * n_e, LANES), 0).astype(F32)
    named = jnp.zeros((2 * n_e, LANES), F32)
    for k in range(8):
        named = jnp.where((placed[k : k + 1] == expert) & own_lane, 1.0, named)
    l_row = lax.broadcasted_iota(jnp.int32, (LANES, LANES), 0)
    l_col = lax.broadcasted_iota(jnp.int32, (LANES, LANES), 1)
    before = jnp.where(l_row < l_col, 1.0, 0.0).astype(BF16)
    count = jnp.dot(named.astype(BF16), before, preferred_element_type=F32)
    ranks = [
        jnp.sum(jnp.where(placed[k : k + 1] == expert, count, 0.0), axis=0, keepdims=True)
        for k in range(8)
    ]
    own_codes = placed[:8] * RPAD + jnp.concatenate(ranks, axis=0)
    codes_own[...] = own_codes
    tile[...] = jnp.concatenate(
        [jnp.where(own_lane, own_codes - CODE_SHIFT, 0.0), placed[8:]], axis=0
    ).astype(BF16)
    for o in range(1, n_x):
        t_copy(o).start()
    tr[xi] = tile[...]
    for o in range(1, n_x):
        h_copy(o).start()

    k_tok = lax.broadcasted_iota(jnp.int32, spread.shape, 0)
    lane = lax.broadcasted_iota(jnp.int32, spread.shape, 1)
    token_of = lane // piece_rows * tok + lane % tok
    spread[...] = jnp.where((token_of == k_tok) & (lane < og_rows), 1.0, 0.0).astype(BF16)
    row = lax.broadcasted_iota(jnp.int32, tgt.shape, 0)
    col = lax.broadcasted_iota(jnp.int32, tgt.shape, 1)
    expert_row = me * 2 + row // rows_x
    tgt[...] = (expert_row * RPAD + row % RPAD).astype(F32) - CODE_SHIFT
    lanemask[...] = jnp.where(col // tok == row // RPAD % n_x, 1.0, 0.0)
    acc[...] = jnp.zeros_like(acc)

    own_x.wait()
    for o in range(1, n_x):
        x_copy(o).wait_recv()
        t_copy(o).wait_recv()
    table = jnp.zeros((16, LANES), F32)
    for x in range(n_x):
        blk[core, me, x * piece_rows : (x + 1) * piece_rows, :] = xr[x]
        table = table + tr[x].astype(F32)
    blk[core, me, og_rows:, :] = table.astype(BF16)

    def hop(h, slot, dist, c, stride):
        ref = blk.at[h, slot, pl.ds(c * chunk, chunk), :]
        to = wrap(me + jnp.where(core == 0, stride, n_e - stride), n_e)
        return remote(ref, ref, z_send.at[h, dist - 1, c], z_recv.at[h, dist - 1, c], {"expert": to})

    def seen(way, dist):
        return wrap(me + jnp.where(way == 0, n_e - dist, dist), n_e)

    def hand_over(slot, i):
        ref = blk.at[1 - core, slot]
        return remote(ref, ref, d_send.at[i], d_recv.at[i], other)

    def handed(slot, i):
        ref = blk.at[core, slot]
        return remote(ref, ref, d_send.at[i], d_recv.at[i], other)

    own_half = blk.at[core, me]
    o_copy = remote(own_half, own_half, o_send, o_recv, other)
    their_half = blk.at[1 - core, me]
    o_arrival = remote(their_half, their_half, o_send, o_recv, other)
    last = half - core

    def order(i):
        mid = jnp.where(i % 2 == 0, JUMP - 1 + i // 2, (i + 3) // 2)
        return jnp.where((i < 2) | (i >= 2 * JUMP - 4), i + 1, mid)

    o_copy.start()
    for c in range(PIECES):
        hop(core, me, 1, c, 1).start()
    o_arrival.wait_recv()
    for c in range(PIECES):
        hop(1 - core, me, 1, c, 1).start()
    for h in range(2):
        for c in range(PIECES):
            hop(h, me, JUMP, c, JUMP).start()

    def pass_on(dist, i):
        slot = seen(core, dist)
        more = (dist != JUMP - 1) & (dist != last)
        for h in (core, 1 - core):
            for c in range(PIECES):
                hop(h, slot, dist, c, 1).wait_recv()

                @pl.when(more)
                def _():
                    hop(h, slot, dist + 1, c, 1).start()

        hand_over(slot, i).start()

    def pair(i):
        far = jnp.where(i >= 1, order(jnp.maximum(i - 1, 0)), 0)
        return seen(1, far), seen(0, order(i))

    own_w.wait()
    w_copy.wait_recv()

    def block_rows(e, i, ab):
        routing = blk[core, e, og_rows:, :].astype(F32)
        codes, gates = routing[:8], routing[8:]
        want, mask = tgt[...], lanemask[...]
        hit = jnp.zeros(tgt.shape, F32)
        gate = jnp.zeros(tgt.shape, F32)
        for k in range(8):
            same = codes[k : k + 1, :] == want
            hit = jnp.where(same, 1.0, hit)
            gate = jnp.where(same, gates[k : k + 1, :], gate)
        gate_col = jnp.sum(gate * mask, axis=1, keepdims=True)
        gate_cols[i, ab] = jnp.broadcast_to(gate_col, tgt.shape)
        wide = jnp.dot((hit * mask).astype(BF16), spread[...], preferred_element_type=F32)
        q_of = lax.broadcasted_iota(jnp.int32, (1, blk_rows), 1) % piece_rows // tok
        pick = jnp.concatenate(
            [jnp.where(q_of == q, wide, 0.0).astype(BF16) for q in range(q_n)], axis=0
        )
        got = jnp.dot(pick, blk[core, e], preferred_element_type=F32)
        got = jnp.concatenate(
            [got[q * 2 * rows_x : (q + 1) * 2 * rows_x] for q in range(q_n)], axis=1
        )
        return got.astype(BF16), (got * gate_col).astype(BF16)

    def compute(i):
        ea, eb = pair(i)
        rows_a, scaled_a = block_rows(ea, i, 0)
        rows_b, scaled_b = block_rows(eb, i, 1)
        parts = []
        for x in range(2):
            cut = slice(x * rows_x, (x + 1) * rows_x)
            scaled_rows[x, i, :rows_x, :] = scaled_a[cut]
            scaled_rows[x, i, rows_x:, :] = scaled_b[cut]
            lhs = jnp.concatenate([rows_a[cut], rows_b[cut]], axis=0)
            parts.append(
                jnp.dot(lhs[:, :fs], w2[0, x], preferred_element_type=F32)
                + jnp.dot(lhs[:, fs:], w2[1, x], preferred_element_type=F32)
            )
        for x in range(n_x):
            tiles = [
                parts[b][ab * rows_x + x * RPAD : ab * rows_x + (x + 1) * RPAD]
                for ab in range(2)
                for b in range(2)
            ]
            p_send[x, i] = jnp.concatenate(tiles, axis=0).astype(BF16)

    def p_copy(o, i):
        t = wrap(xi + o, n_x)
        return remote(
            p_send.at[t, i], p_recv.at[xi, i], ps_send.at[o - 1, i], ps_recv.at[o - 1, i], x_dev(t)
        )

    def g_copy(o):
        t = wrap(me + o, n_e)
        return remote(gs.at[t], gr.at[me], g_send.at[o], g_recv.at[o], {"expert": t})

    def combine(i):
        for o in range(1, n_x):
            p_copy(o, i).wait_recv()
        total = p_send[xi, i].astype(F32)
        for o in range(1, n_x):
            total = total + p_recv[wrap(xi + n_x - o, n_x), i].astype(F32)
        for ab in range(2):
            e = pair(i)[ab]
            part = total[ab * 16 : (ab + 1) * 16]
            gate = jnp.concatenate(
                [gate_cols[i, ab, pl.ds(pl.multiple_of(x * rows_x + xi * RPAD, RPAD), RPAD), :] for x in range(2)],
                axis=0,
            )
            hg_out[e] = (gate[:, :1] * part).astype(BF16)
            grad = jnp.sum(part * hp[e].astype(F32), axis=1, keepdims=True)
            r16 = lax.broadcasted_iota(jnp.int32, (16, LANES), 0)
            l16 = lax.broadcasted_iota(jnp.int32, (16, LANES), 1)
            line = jnp.where(l16 == r16, grad, 0.0)
            gs[e] = jnp.sum(line, axis=0, keepdims=True)

        g_copy(n_e - order(i)).start()

        @pl.when(i >= 1)
        def _():
            g_copy(order(jnp.maximum(i - 1, 0))).start()

    def grad_step(j):
        for x in range(2):
            lhs, rhs = [], []
            for u in range(2):
                i = 2 * j + u
                lhs.append(scaled_rows[x, i])
                for ab in range(2):
                    e = pair(i)[ab]
                    for s in range(n_x):
                        rhs.append(hidr[s, e].astype(F32)[x * RPAD : (x + 1) * RPAD])
            lhs = jnp.concatenate(lhs, axis=0)
            rhs = jnp.concatenate(rhs, axis=0).astype(BF16)
            acc[x] += lax.dot_general(lhs, rhs, (((0,), (0,)), ((), ())), preferred_element_type=F32)

    def work(i):
        ea, eb = pair(i)

        @pl.when(core == 1)
        def _():
            handed(eb, i).wait_recv()

        @pl.when((core == 0) & (i >= 1))
        def _():
            handed(ea, i - 1).wait_recv()

        compute(i)
        for o in range(1, n_x):
            p_copy(o, i).start()

        @pl.when(i >= half // 2)
        def _():
            combine(i - half // 2)

        @pl.when(i >= 3 * half // 4)
        def _():
            combine(i - half // 4)

        @pl.when(i == half // 2)
        def _():
            own_h.wait()
            for o in range(1, n_x):
                h_copy(o).wait_recv()

        @pl.when(i >= half // 2)
        def _():
            grad_step(i - half // 2)

    @pl.loop(0, half)
    def _(i):
        @pl.when(i < last)
        def _():
            pass_on(order(i), i)

        @pl.when(i >= 1)
        def _():
            work(i - 1)

    work(half - 1)

    cut = fs // n_p

    def c_copy(x):
        return remote(ws.at[x], wc.at[x], c_send.at[x], c_recv.at[x], other)

    def r_copy(o, x):
        t = wrap(p + o, n_p)
        return remote(wd.at[t, x], wr.at[p, x], r_send.at[o - 1, x], r_recv.at[o - 1, x], {"dp": t})

    def a_copy(o, x, src):
        at = wag.at[src, x]
        return remote(at, at, a_send.at[o - 1, x], a_recv.at[o - 1, x], {"dp": wrap(p + o, n_p)})

    def summed(t, x):
        at = pl.multiple_of(core * fs + t * cut, cut)
        return acc[x, pl.ds(at, cut), :] + wc[x, pl.ds(pl.multiple_of(t * cut, cut), cut), :].astype(F32)

    for x in range(2):
        ws[x] = acc[x, pl.ds(pl.multiple_of((1 - core) * fs, fs), fs), :].astype(BF16)
        c_copy(x).start()

    @pl.loop(3 * half // 4, half)
    def _(i):
        combine(i)

    gr[me] = gs[me]
    for x in range(2):
        c_copy(x).wait_recv()
        for o in range(1, n_p):
            t = wrap(p + o, n_p)
            wd[t, x] = summed(t, x).astype(BF16)
            r_copy(o, x).start()

    for x in range(2):
        mine = summed(p, x)
        for o in range(1, n_p):
            r_copy(o, x).wait_recv()
            mine = mine + wr[wrap(p + n_p - o, n_p), x].astype(F32)
        wag[p, x] = mine.astype(BF16)
        for o in range(1, n_p):
            a_copy(o, x, p).start()

    @pl.loop(1, n_e)
    def _(o):
        g_copy(o).wait_recv()

    own = codes_own[...].astype(jnp.int32)
    e_of = lax.broadcasted_iota(jnp.int32, (n_e, LANES), 0)
    one = jnp.concatenate(
        [jnp.where(e_of == own[k : k + 1] // 16, 1.0, 0.0) for k in range(8)], axis=1
    )
    got = lax.dot_general(
        gr[:, 0, :], one, (((0,), (0,)), ((), ())),
        preferred_element_type=F32, precision=lax.Precision.HIGHEST,
    )[:16]
    s_of = lax.broadcasted_iota(jnp.int32, (16, LANES), 0)
    lines = [
        jnp.sum(
            jnp.where(s_of == own[k : k + 1] % 16, got[:, k * LANES : (k + 1) * LANES], 0.0),
            axis=0, keepdims=True,
        )
        for k in range(8)
    ]
    gg_out[...] = lax.dot_general(
        jnp.concatenate(lines, axis=0), place, (((1,), (1,)), ((), ())),
        preferred_element_type=F32, precision=lax.Precision.HIGHEST,
    )

    for x in range(2):
        wg_out[x, pl.ds(pl.multiple_of(p * cut, cut), cut), :] = wag[p, x].astype(F32)
        for o in range(1, n_p):
            src = wrap(p + n_p - o, n_p)
            a_copy(o, x, src).wait_recv()
            wg_out[x, pl.ds(pl.multiple_of(src * cut, cut), cut), :] = wag[src, x].astype(F32)

    for o in range(1, n_x):
        x_copy(o).wait_send()
        t_copy(o).wait_send()
        h_copy(o).wait_send()
    w_copy.wait_send()
    for x in range(2):
        c_copy(x).wait_send()
        for o in range(1, n_p):
            r_copy(o, x).wait_send()
            a_copy(o, x, p).wait_send()

    @pl.loop(1, n_e)
    def _(o):
        g_copy(o).wait_send()

    @pl.loop(0, half)
    def _(i):
        for o in range(1, n_x):
            p_copy(o, i).wait_send()

        @pl.when(i < last)
        def _():
            hand_over(me, i).wait_send()
            for h in range(2):
                for c in range(PIECES):
                    hop(h, me, i + 1, c, 1).wait_send()

    o_copy.wait_send()


def shards(n_e, n_x, n_p, out_grad, gates, routes, hidden_acts, w_down):
    tok, top = routes.shape
    exp_dev = w_down.shape[1]
    fs = w_down.shape[0]
    width = w_down.shape[2]
    slot = hidden_acts.shape[1] // n_e
    half = n_e // 2
    chip_cols = 2 * fs
    q_n = chip_cols // LANES
    piece_rows = q_n * tok
    blk_rows = n_x * piece_rows + 16
    rows_x = n_x * RPAD

    pre = out_grad.reshape(tok, n_x, q_n, LANES).transpose(1, 2, 0, 3).reshape(n_x, piece_rows, LANES)
    hp = hidden_acts.reshape(exp_dev, n_e, slot, width).transpose(1, 0, 2, 3)
    hp = jnp.pad(hp, ((0, 0), (0, 0), (0, RPAD - slot), (0, 0))).reshape(n_e, 2 * RPAD, width)
    wt = w_down.transpose(1, 0, 2)

    dma = pltpu.SemaphoreType.DMA
    vmem = pl.BlockSpec(memory_space=pltpu.VMEM)
    cut = fs // n_p
    hg, gg, wg = pl.pallas_call(
        functools.partial(kernel, n_e, n_x, n_p, tok),
        out_shape=(
            jax.ShapeDtypeStruct((n_e, 2 * RPAD, width), BF16),
            jax.ShapeDtypeStruct((top, tok), F32),
            jax.ShapeDtypeStruct((exp_dev, fs, width), F32),
        ),
        in_specs=[vmem] * 5,
        out_specs=(vmem,) * 3,
        scratch_shapes=[
            pltpu.VMEM((2, n_e, blk_rows, LANES), BF16),
            pltpu.VMEM((n_x, piece_rows, LANES), BF16),
            pltpu.VMEM((16, LANES), BF16),
            pltpu.VMEM((n_x, 16, LANES), BF16),
            pltpu.VMEM((8, LANES), F32),
            pltpu.VMEM((n_x, n_e, 2 * RPAD, width), BF16),
            pltpu.VMEM((2, exp_dev, fs, width), BF16),
            pltpu.VMEM((LANES, blk_rows), BF16),
            pltpu.VMEM((2 * rows_x, LANES), F32),
            pltpu.VMEM((2 * rows_x, LANES), F32),
            pltpu.VMEM((n_x, half, 4 * RPAD, width), BF16),
            pltpu.VMEM((n_x, half, 4 * RPAD, width), BF16),
            pltpu.VMEM((2, half, 2 * rows_x, chip_cols), BF16),
            pltpu.VMEM((half, 2, 2 * rows_x, LANES), F32),
            pltpu.VMEM((2, chip_cols, width), F32),
            pltpu.VMEM((n_e, 1, LANES), F32),
            pltpu.VMEM((n_e, 1, LANES), F32),
            pltpu.VMEM((2, fs, width), BF16),
            pltpu.VMEM((2, fs, width), BF16),
            pltpu.VMEM((n_p, 2, cut, width), BF16),
            pltpu.VMEM((n_p, 2, cut, width), BF16),
            pltpu.VMEM((n_p, 2, cut, width), BF16),
            dma((n_x - 1,)), dma((n_x - 1,)), dma((n_x - 1,)), dma((n_x - 1,)), dma((n_x - 1,)), dma((n_x - 1,)),
            dma, dma, dma((3,)),
            dma((2, half, PIECES)), dma((2, half, PIECES)), dma((half,)), dma((half,)), dma, dma,
            dma((n_x - 1, half)), dma((n_x - 1, half)),
            dma((n_e,)), dma((n_e,)), dma((2,)), dma((2,)),
            dma((n_p - 1, 2)), dma((n_p - 1, 2)), dma((n_p - 1, 2)), dma((n_p - 1, 2)),
        ],
        compiler_params=pltpu.CompilerParams(
            collective_id=0, has_side_effects=True, vmem_limit_bytes=40 * 1024 * 1024
        ),
    )(pre, routes.T, gates.T, hp, wt)
    hg = hg.reshape(n_e, exp_dev, RPAD, width)[:, :, :slot].transpose(1, 0, 2, 3)
    return hg.reshape(exp_dev, n_e * slot, width), gg.T, wg.transpose(1, 0, 2)


def solution(mesh):
    n_x = mesh.shape["fsdp"] // 2
    in_specs = (
        P(("expert", "fsdp", "dp"), None),
        P(("expert", "fsdp", "dp"), None),
        P(("expert", "fsdp", "dp"), None),
        P("expert", ("fsdp", "dp"), None),
        P("fsdp", "expert", None),
    )
    out_specs = (
        P("expert", ("fsdp", "dp"), None),
        P(("expert", "fsdp", "dp"), None),
        P("fsdp", "expert", None),
    )
    return jax.shard_map(
        functools.partial(shards, mesh.shape["expert"], n_x, mesh.shape["dp"]),
        mesh=mesh,
        in_specs=in_specs,
        out_specs=out_specs,
        check_vma=False,
    )
```

```python
import functools

import jax
import jax.numpy as jnp
from jax import lax
from jax.experimental import pallas as pl
from jax.experimental.pallas import tpu as pltpu
from jax.sharding import PartitionSpec as P

MESH = pl.DeviceIdType.MESH
F32 = jnp.float32
BF16 = jnp.bfloat16
LANES = 128
RPAD = 8
CODE_SHIFT = 256.0
PIECES = 3
JUMP = 8


def remote(src, dst, send, recv, where):
    return pltpu.make_async_remote_copy(
        src_ref=src, dst_ref=dst, send_sem=send, recv_sem=recv, device_id=where, device_id_type=MESH
    )


def kernel(
    n_e, n_x, n_p, tok,
    pre, routes, gates, hp, wt, hg_out, gg_out, wg_out,
    blk, xr, tile, tr, codes_own, hidr, w2, spread, tgt, lanemask, p_send, p_recv, scaled_rows, gate_cols, acc,
    gs, gr, ws, wc, wd, wr, wag,
    x_send, x_recv, t_send, t_recv, h_send, h_recv, w_send, w_recv, loc,
    z_send, z_recv, ps_send, ps_recv, g_send, g_recv, c_send, c_recv, r_send, r_recv, a_send, a_recv,
):
    me = lax.axis_index("expert")
    f = lax.axis_index("fsdp")
    p = lax.axis_index("dp")
    xi, core = f // 2, f % 2
    half = n_e // 2
    piece_rows = pre.shape[1]
    og_rows = n_x * piece_rows
    blk_rows = og_rows + 16
    q_n = piece_rows // tok
    chunk = blk_rows // PIECES
    width = hp.shape[2]
    fs = wt.shape[1]
    rows_x = n_x * RPAD

    def x_dev(t):
        return {"fsdp": t * 2 + core}

    other = {"fsdp": xi * 2 + 1 - core}

    barrier = pltpu.get_barrier_semaphore()

    for o in (1, n_e - 1, JUMP, n_e - JUMP):
        pl.semaphore_signal(barrier, inc=1, device_id={"expert": (me + o) % n_e}, device_id_type=MESH)
    for o in range(1, n_x):
        pl.semaphore_signal(barrier, inc=1, device_id=x_dev((xi + o) % n_x), device_id_type=MESH)
    pl.semaphore_signal(barrier, inc=1, device_id=other, device_id_type=MESH)
    for o in range(1, n_p):
        pl.semaphore_signal(barrier, inc=1, device_id={"dp": (p + o) % n_p}, device_id_type=MESH)
    pl.semaphore_wait(barrier, 4 + (n_x - 1) + 1 + (n_p - 1))

    def x_copy(o):
        t = (xi + o) % n_x
        return remote(pre.at[t], xr.at[xi], x_send.at[o - 1], x_recv.at[o - 1], x_dev(t))

    def t_copy(o):
        t = (xi + o) % n_x
        return remote(tile, tr.at[xi], t_send.at[o - 1], t_recv.at[o - 1], x_dev(t))

    def h_copy(o):
        t = (xi + o) % n_x
        return remote(hp, hidr.at[xi], h_send.at[o - 1], h_recv.at[o - 1], x_dev(t))

    w_copy = remote(wt, w2.at[core], w_send, w_recv, other)
    own_w = pltpu.make_async_copy(wt, w2.at[core], loc.at[0])
    own_h = pltpu.make_async_copy(hp, hidr.at[xi], loc.at[1])
    own_x = pltpu.make_async_copy(pre.at[xi], xr.at[xi], loc.at[2])

    for o in range(1, n_x):
        x_copy(o).start()
    own_x.start()
    w_copy.start()
    own_w.start()
    own_h.start()

    t_row = lax.broadcasted_iota(jnp.int32, (tok, LANES), 0)
    t_col = lax.broadcasted_iota(jnp.int32, (tok, LANES), 1)
    place = jnp.where(t_col == xi * tok + t_row, 1.0, 0.0)
    both = jnp.concatenate(
        [routes[...].astype(F32), gates[...].astype(BF16).astype(F32)], axis=0
    ).astype(BF16)
    placed = jnp.dot(both, place.astype(BF16), preferred_element_type=F32)
    own_lane = lax.broadcasted_iota(jnp.int32, (1, LANES), 1) // tok == xi
    expert = lax.broadcasted_iota(jnp.int32, (2 * n_e, LANES), 0).astype(F32)
    named = jnp.zeros((2 * n_e, LANES), F32)
    for k in range(8):
        named = jnp.where((placed[k : k + 1] == expert) & own_lane, 1.0, named)
    l_row = lax.broadcasted_iota(jnp.int32, (LANES, LANES), 0)
    l_col = lax.broadcasted_iota(jnp.int32, (LANES, LANES), 1)
    before = jnp.where(l_row < l_col, 1.0, 0.0).astype(BF16)
    count = jnp.dot(named.astype(BF16), before, preferred_element_type=F32)
    ranks = [
        jnp.sum(jnp.where(placed[k : k + 1] == expert, count, 0.0), axis=0, keepdims=True)
        for k in range(8)
    ]
    own_codes = placed[:8] * RPAD + jnp.concatenate(ranks, axis=0)
    codes_own[...] = own_codes
    tile[...] = jnp.concatenate(
        [jnp.where(own_lane, own_codes - CODE_SHIFT, 0.0), placed[8:]], axis=0
    ).astype(BF16)
    for o in range(1, n_x):
        t_copy(o).start()
    tr[xi] = tile[...]
    for o in range(1, n_x):
        h_copy(o).start()

    k_tok = lax.broadcasted_iota(jnp.int32, spread.shape, 0)
    lane = lax.broadcasted_iota(jnp.int32, spread.shape, 1)
    token_of = lane // piece_rows * tok + lane % tok
    spread[...] = jnp.where((token_of == k_tok) & (lane < og_rows), 1.0, 0.0).astype(BF16)
    row = lax.broadcasted_iota(jnp.int32, tgt.shape, 0)
    col = lax.broadcasted_iota(jnp.int32, tgt.shape, 1)
    expert_row = me * 2 + row // rows_x
    tgt[...] = (expert_row * RPAD + row % RPAD).astype(F32) - CODE_SHIFT
    lanemask[...] = jnp.where(col // tok == row // RPAD % n_x, 1.0, 0.0)
    acc[...] = jnp.zeros_like(acc)

    own_x.wait()
    for o in range(1, n_x):
        x_copy(o).wait_recv()
        t_copy(o).wait_recv()
    table = jnp.zeros((16, LANES), F32)
    for x in range(n_x):
        blk[me, x * piece_rows : (x + 1) * piece_rows, :] = xr[x]
        table = table + tr[x].astype(F32)
    blk[me, og_rows:, :] = table.astype(BF16)

    def hop(way, slot, dist, c, stride):
        ref = blk.at[slot, pl.ds(c * chunk, chunk), :]
        to = (me + stride) % n_e if way == 0 else (me + n_e - stride) % n_e
        return remote(ref, ref, z_send.at[way, dist - 1, c], z_recv.at[way, dist - 1, c], {"expert": to})

    def seen(way, dist):
        return (me + n_e - dist) % n_e if way == 0 else (me + dist) % n_e

    def order(i):
        mid = jnp.where(i % 2 == 0, JUMP - 1 + i // 2, (i + 3) // 2)
        return jnp.where((i < 2) | (i >= 2 * JUMP - 4), i + 1, mid)

    for c in range(PIECES):
        for way in range(2):
            hop(way, me, 1, c, 1).start()
    for c in range(PIECES):
        for way in range(2):
            hop(way, me, JUMP, c, JUMP).start()

    def pass_on(way, dist, c, last):
        hop(way, seen(way, dist), dist, c, 1).wait_recv()

        @pl.when((dist != JUMP - 1) & (dist != last))
        def _():
            hop(way, seen(way, dist), dist + 1, c, 1).start()

    def pair(i):
        far = jnp.where(i >= 1, order(jnp.maximum(i - 1, 0)), 0)
        return seen(1, far), seen(0, order(i))

    own_w.wait()
    w_copy.wait_recv()

    def block_rows(e, i, ab):
        routing = blk[e, og_rows:, :].astype(F32)
        codes, gates = routing[:8], routing[8:]
        want, mask = tgt[...], lanemask[...]
        hit = jnp.zeros(tgt.shape, F32)
        gate = jnp.zeros(tgt.shape, F32)
        for k in range(8):
            same = codes[k : k + 1, :] == want
            hit = jnp.where(same, 1.0, hit)
            gate = jnp.where(same, gates[k : k + 1, :], gate)
        gate_col = jnp.sum(gate * mask, axis=1, keepdims=True)
        gate_cols[i, ab] = jnp.broadcast_to(gate_col, tgt.shape)
        wide = jnp.dot((hit * mask).astype(BF16), spread[...], preferred_element_type=F32)
        q_of = lax.broadcasted_iota(jnp.int32, (1, blk_rows), 1) % piece_rows // tok
        pick = jnp.concatenate(
            [jnp.where(q_of == q, wide, 0.0).astype(BF16) for q in range(q_n)], axis=0
        )
        got = jnp.dot(pick, blk[e], preferred_element_type=F32)
        got = jnp.concatenate(
            [got[q * 2 * rows_x : (q + 1) * 2 * rows_x] for q in range(q_n)], axis=1
        )
        return got.astype(BF16), (got * gate_col).astype(BF16)

    def compute(i):
        ea, eb = pair(i)
        rows_a, scaled_a = block_rows(ea, i, 0)
        rows_b, scaled_b = block_rows(eb, i, 1)
        parts = []
        for x in range(2):
            cut = slice(x * rows_x, (x + 1) * rows_x)
            scaled_rows[x, i, :rows_x, :] = scaled_a[cut]
            scaled_rows[x, i, rows_x:, :] = scaled_b[cut]
            lhs = jnp.concatenate([rows_a[cut], rows_b[cut]], axis=0)
            parts.append(
                jnp.dot(lhs[:, :fs], w2[0, x], preferred_element_type=F32)
                + jnp.dot(lhs[:, fs:], w2[1, x], preferred_element_type=F32)
            )
        for x in range(n_x):
            tiles = [
                parts[b][ab * rows_x + x * RPAD : ab * rows_x + (x + 1) * RPAD]
                for ab in range(2)
                for b in range(2)
            ]
            p_send[x, i] = jnp.concatenate(tiles, axis=0).astype(BF16)

    def p_copy(o, i):
        t = (xi + o) % n_x
        return remote(
            p_send.at[t, i], p_recv.at[xi, i], ps_send.at[o - 1, i], ps_recv.at[o - 1, i], x_dev(t)
        )

    def g_copy(o):
        t = (me + o) % n_e
        return remote(gs.at[t], gr.at[me], g_send.at[o], g_recv.at[o], {"expert": t})

    def combine(i):
        for o in range(1, n_x):
            p_copy(o, i).wait_recv()
        total = p_send[xi, i].astype(F32)
        for o in range(1, n_x):
            total = total + p_recv[(xi + n_x - o) % n_x, i].astype(F32)
        for ab in range(2):
            e = pair(i)[ab]
            part = total[ab * 16 : (ab + 1) * 16]
            gate = jnp.concatenate(
                [gate_cols[i, ab, pl.ds(pl.multiple_of(x * rows_x + xi * RPAD, RPAD), RPAD), :] for x in range(2)],
                axis=0,
            )
            hg_out[e] = (gate[:, :1] * part).astype(BF16)
            grad = jnp.sum(part * hp[e].astype(F32), axis=1, keepdims=True)
            r16 = lax.broadcasted_iota(jnp.int32, (16, LANES), 0)
            l16 = lax.broadcasted_iota(jnp.int32, (16, LANES), 1)
            line = jnp.where(l16 == r16, grad, 0.0)
            gs[e] = jnp.sum(line, axis=0, keepdims=True)

        g_copy(n_e - order(i)).start()

        @pl.when(i >= 1)
        def _():
            g_copy(order(jnp.maximum(i - 1, 0))).start()

    def grad_step(j):
        for x in range(2):
            lhs, rhs = [], []
            for u in range(2):
                i = 2 * j + u
                lhs.append(scaled_rows[x, i])
                for ab in range(2):
                    e = pair(i)[ab]
                    for s in range(n_x):
                        rhs.append(hidr[s, e].astype(F32)[x * RPAD : (x + 1) * RPAD])
            lhs = jnp.concatenate(lhs, axis=0)
            rhs = jnp.concatenate(rhs, axis=0).astype(BF16)
            acc[x] += lax.dot_general(lhs, rhs, (((0,), (0,)), ((), ())), preferred_element_type=F32)

    @pl.loop(0, half)
    def _(i):
        for c in range(PIECES):
            pass_on(0, order(i), c, half)

            @pl.when(i >= 1)
            def _():
                pass_on(1, order(jnp.maximum(i - 1, 0)), c, half - 1)

        compute(i)
        for o in range(1, n_x):
            p_copy(o, i).start()

        @pl.when(i >= half // 2)
        def _():
            combine(i - half // 2)

        @pl.when(i >= 3 * half // 4)
        def _():
            combine(i - half // 4)

        @pl.when(i == half // 2)
        def _():
            own_h.wait()
            for o in range(1, n_x):
                h_copy(o).wait_recv()

        @pl.when(i >= half // 2)
        def _():
            grad_step(i - half // 2)

    cut = fs // n_p

    def c_copy(x):
        return remote(ws.at[x], wc.at[x], c_send.at[x], c_recv.at[x], other)

    def r_copy(o, x):
        t = (p + o) % n_p
        return remote(wd.at[t, x], wr.at[p, x], r_send.at[o - 1, x], r_recv.at[o - 1, x], {"dp": t})

    def a_copy(o, x, src):
        at = wag.at[src, x]
        return remote(at, at, a_send.at[o - 1, x], a_recv.at[o - 1, x], {"dp": (p + o) % n_p})

    def summed(t, x):
        at = pl.multiple_of(core * fs + t * cut, cut)
        return acc[x, pl.ds(at, cut), :] + wc[x, pl.ds(pl.multiple_of(t * cut, cut), cut), :].astype(F32)

    for x in range(2):
        ws[x] = acc[x, pl.ds(pl.multiple_of((1 - core) * fs, fs), fs), :].astype(BF16)
        c_copy(x).start()
    for x in range(2):
        c_copy(x).wait_recv()
        for o in range(1, n_p):
            t = (p + o) % n_p
            wd[t, x] = summed(t, x).astype(BF16)
            r_copy(o, x).start()

    @pl.loop(3 * half // 4, half)
    def _(i):
        combine(i)

    gr[me] = gs[me]
    for x in range(2):
        mine = summed(p, x)
        for o in range(1, n_p):
            r_copy(o, x).wait_recv()
            mine = mine + wr[(p + n_p - o) % n_p, x].astype(F32)
        wag[p, x] = mine.astype(BF16)
        for o in range(1, n_p):
            a_copy(o, x, p).start()

    @pl.loop(1, n_e)
    def _(o):
        g_copy(o).wait_recv()

    own = codes_own[...].astype(jnp.int32)
    e_of = lax.broadcasted_iota(jnp.int32, (n_e, LANES), 0)
    one = jnp.concatenate(
        [jnp.where(e_of == own[k : k + 1] // 16, 1.0, 0.0) for k in range(8)], axis=1
    )
    got = lax.dot_general(
        gr[:, 0, :], one, (((0,), (0,)), ((), ())),
        preferred_element_type=F32, precision=lax.Precision.HIGHEST,
    )[:16]
    s_of = lax.broadcasted_iota(jnp.int32, (16, LANES), 0)
    lines = [
        jnp.sum(
            jnp.where(s_of == own[k : k + 1] % 16, got[:, k * LANES : (k + 1) * LANES], 0.0),
            axis=0, keepdims=True,
        )
        for k in range(8)
    ]
    gg_out[...] = lax.dot_general(
        jnp.concatenate(lines, axis=0), place, (((1,), (1,)), ((), ())),
        preferred_element_type=F32, precision=lax.Precision.HIGHEST,
    )

    for x in range(2):
        wg_out[x, pl.ds(pl.multiple_of(p * cut, cut), cut), :] = wag[p, x].astype(F32)
        for o in range(1, n_p):
            src = (p + n_p - o) % n_p
            a_copy(o, x, src).wait_recv()
            wg_out[x, pl.ds(pl.multiple_of(src * cut, cut), cut), :] = wag[src, x].astype(F32)

    for o in range(1, n_x):
        x_copy(o).wait_send()
        t_copy(o).wait_send()
        h_copy(o).wait_send()
    w_copy.wait_send()
    for x in range(2):
        c_copy(x).wait_send()
        for o in range(1, n_p):
            r_copy(o, x).wait_send()
            a_copy(o, x, p).wait_send()

    @pl.loop(1, n_e)
    def _(o):
        g_copy(o).wait_send()

    @pl.loop(0, half)
    def _(i):
        for o in range(1, n_x):
            p_copy(o, i).wait_send()
        for c in range(PIECES):
            hop(0, me, i + 1, c, 1).wait_send()

            @pl.when(i < half - 1)
            def _():
                hop(1, me, i + 1, c, 1).wait_send()


def shards(n_e, n_x, n_p, out_grad, gates, routes, hidden_acts, w_down):
    tok, top = routes.shape
    exp_dev = w_down.shape[1]
    fs = w_down.shape[0]
    width = w_down.shape[2]
    slot = hidden_acts.shape[1] // n_e
    half = n_e // 2
    chip_cols = 2 * fs
    q_n = chip_cols // LANES
    piece_rows = q_n * tok
    blk_rows = n_x * piece_rows + 16
    rows_x = n_x * RPAD

    pre = out_grad.reshape(tok, n_x, q_n, LANES).transpose(1, 2, 0, 3).reshape(n_x, piece_rows, LANES)
    hp = hidden_acts.reshape(exp_dev, n_e, slot, width).transpose(1, 0, 2, 3)
    hp = jnp.pad(hp, ((0, 0), (0, 0), (0, RPAD - slot), (0, 0))).reshape(n_e, 2 * RPAD, width)
    wt = w_down.transpose(1, 0, 2)

    dma = pltpu.SemaphoreType.DMA
    vmem = pl.BlockSpec(memory_space=pltpu.VMEM)
    cut = fs // n_p
    hg, gg, wg = pl.pallas_call(
        functools.partial(kernel, n_e, n_x, n_p, tok),
        out_shape=(
            jax.ShapeDtypeStruct((n_e, 2 * RPAD, width), BF16),
            jax.ShapeDtypeStruct((top, tok), F32),
            jax.ShapeDtypeStruct((exp_dev, fs, width), F32),
        ),
        in_specs=[vmem] * 5,
        out_specs=(vmem,) * 3,
        scratch_shapes=[
            pltpu.VMEM((n_e, blk_rows, LANES), BF16),
            pltpu.VMEM((n_x, piece_rows, LANES), BF16),
            pltpu.VMEM((16, LANES), BF16),
            pltpu.VMEM((n_x, 16, LANES), BF16),
            pltpu.VMEM((8, LANES), F32),
            pltpu.VMEM((n_x, n_e, 2 * RPAD, width), BF16),
            pltpu.VMEM((2, exp_dev, fs, width), BF16),
            pltpu.VMEM((LANES, blk_rows), BF16),
            pltpu.VMEM((2 * rows_x, LANES), F32),
            pltpu.VMEM((2 * rows_x, LANES), F32),
            pltpu.VMEM((n_x, half, 4 * RPAD, width), BF16),
            pltpu.VMEM((n_x, half, 4 * RPAD, width), BF16),
            pltpu.VMEM((2, half, 2 * rows_x, chip_cols), BF16),
            pltpu.VMEM((half, 2, 2 * rows_x, LANES), F32),
            pltpu.VMEM((2, chip_cols, width), F32),
            pltpu.VMEM((n_e, 1, LANES), F32),
            pltpu.VMEM((n_e, 1, LANES), F32),
            pltpu.VMEM((2, fs, width), BF16),
            pltpu.VMEM((2, fs, width), BF16),
            pltpu.VMEM((n_p, 2, cut, width), BF16),
            pltpu.VMEM((n_p, 2, cut, width), BF16),
            pltpu.VMEM((n_p, 2, cut, width), BF16),
            dma((n_x - 1,)), dma((n_x - 1,)), dma((n_x - 1,)), dma((n_x - 1,)), dma((n_x - 1,)), dma((n_x - 1,)),
            dma, dma, dma((3,)),
            dma((2, half, PIECES)), dma((2, half, PIECES)),
            dma((n_x - 1, half)), dma((n_x - 1, half)),
            dma((n_e,)), dma((n_e,)), dma((2,)), dma((2,)),
            dma((n_p - 1, 2)), dma((n_p - 1, 2)), dma((n_p - 1, 2)), dma((n_p - 1, 2)),
        ],
        compiler_params=pltpu.CompilerParams(
            collective_id=0, has_side_effects=True, vmem_limit_bytes=40 * 1024 * 1024
        ),
    )(pre, routes.T, gates.T, hp, wt)
    hg = hg.reshape(n_e, exp_dev, RPAD, width)[:, :, :slot].transpose(1, 0, 2, 3)
    return hg.reshape(exp_dev, n_e * slot, width), gg.T, wg.transpose(1, 0, 2)


def solution(mesh):
    n_x = mesh.shape["fsdp"] // 2
    in_specs = (
        P(("expert", "fsdp", "dp"), None),
        P(("expert", "fsdp", "dp"), None),
        P(("expert", "fsdp", "dp"), None),
        P("expert", ("fsdp", "dp"), None),
        P("fsdp", "expert", None),
    )
    out_specs = (
        P("expert", ("fsdp", "dp"), None),
        P(("expert", "fsdp", "dp"), None),
        P("fsdp", "expert", None),
    )
    return jax.shard_map(
        functools.partial(shards, mesh.shape["expert"], n_x, mesh.shape["dp"]),
        mesh=mesh,
        in_specs=in_specs,
        out_specs=out_specs,
        check_vma=False,
    )
```
